512 devices in a mesh: section: 2 (over x_lo), row: 16 (over y, core), col: 16 (over z, x_hi).
Axes of the slice: x: 4 (x_hi: 2, x_lo: 2; x = x_hi * 2 + x_lo), y: 8, z: 8, core: 2. Of those that a mesh axis runs over, the one named last changes fastest.
Arguments:
- activations: bfloat16 [2, 512, 6144], P('section', 'col', 'row'), may hold values from -6 to 6
- weights: bfloat16 [2, 6144, 24576], P('section', 'row', 'col'), may hold values from -0.078125 to 0.078125
Outputs:
- boundary: bfloat16 [2, 512, 6144], P('section', 'col', 'row')
- weight_grads: bfloat16 [2, 6144, 24576], P('section', 'row', 'col')
The draws below stay inside these ranges and needn't reach their ends.
All inputs are finite; a program needn't handle non-finite values.
Results may differ from the reference program's by a relative error of at most 0.034.
Values may be sent and summed in bfloat16 or wider, within the bound.
No kernel may reach another device: no remote copies, remote signals or barrier semaphores. Data moves between devices by JAX's collectives and lax.ppermute only.
A program may use at most 64 MiB of HBM per device.

```python
import jax
import jax.numpy as jnp
from jax import lax

D = 6144
FF = 24576
TOKENS = 512
N_ROW = 16
N_COL = 16


def steps_of(key, extent, shards, smallest, high):
    def one(axis_at, blocks):
        steps = jax.random.uniform(jax.random.fold_in(jax.random.fold_in(key, 6), axis_at), (blocks,), jnp.float32, smallest / len(shards), high / len(shards))
        return jnp.repeat(jnp.exp(steps), extent[axis_at] // blocks).reshape((-1,) + (1,) * (len(extent) - axis_at - 1))

    loudness = one(*shards[0])
    for cut in shards[1:]:
        loudness = loudness * one(*cut)
    return loudness


def bell_draw(stream_key, shape, scale, bound, cuts=(), kind=jnp.bfloat16):
    values = scale * jax.random.normal(stream_key, shape, jnp.float32)
    if cuts:
        values = values * steps_of(stream_key, shape, cuts, -0.22, 0.18)
    return jnp.clip(values, -bound, bound).astype(kind)


def setup_inputs(seed: int = 0) -> dict:
    key_list = jax.random.split(jax.random.key(seed), 3)
    activations = bell_draw(key_list[0], (2, TOKENS, D), 1.0, 6.0, ((0, 2), (1, 16), (2, 16)))
    weights = bell_draw(key_list[1], (2, D, FF), D ** -0.5, 0.078125, ((0, 2), (1, 16), (2, 16)))
    return dict(activations=activations, weights=weights)


gelu_scale = 0.7978845608028654
cubic_coef = 0.044715


def gelu_value(preact):
    inner = gelu_scale * (preact + cubic_coef * preact * preact * preact)
    return 0.5 * preact * (1.0 + jnp.tanh(inner))


def gelu_slope(preact):
    inner = gelu_scale * (preact + cubic_coef * preact * preact * preact)
    tangent = jnp.tanh(inner)
    return 0.5 * (1.0 + tangent) + 0.5 * preact * (1.0 - tangent * tangent) * gelu_scale * (1.0 + 3.0 * cubic_coef * preact * preact)


def blocked_sum(left, right, blocks):
    span = left.shape[1] // blocks

    def step(summed, position):
        offset = (position * span).astype(jnp.int32)
        piece_left = lax.dynamic_slice_in_dim(left, offset, span, 1)
        piece_right = lax.dynamic_slice_in_dim(right, offset, span, 0)
        term = jnp.dot(piece_left, piece_right, preferred_element_type=jnp.float32)
        return summed + term.astype(jnp.bfloat16).astype(jnp.float32), None

    start_value = jnp.zeros((left.shape[0], right.shape[1]), jnp.float32)
    summed, unused = lax.scan(step, start_value, jnp.arange(blocks, dtype=jnp.int32))
    return summed


def reference(activations, weights):
    inputs = activations[0]
    out_grad = activations[1]
    w_up = weights[0]
    w_down_t = weights[1]
    preact = blocked_sum(inputs, w_up, N_ROW)
    hidden = gelu_value(preact).astype(jnp.bfloat16)
    dhidden = blocked_sum(out_grad, w_down_t, N_ROW).astype(jnp.bfloat16)
    dpre = (dhidden.astype(jnp.float32) * gelu_slope(preact)).astype(jnp.bfloat16)
    grad_up = jnp.dot(inputs.T, dpre, preferred_element_type=jnp.float32).astype(jnp.bfloat16)
    grad_down = jnp.dot(out_grad.T, hidden, preferred_element_type=jnp.float32).astype(jnp.bfloat16)
    input_grad = blocked_sum(dpre, w_up.T, N_COL).astype(jnp.bfloat16)
    output_again = blocked_sum(hidden, w_down_t.T, N_COL).astype(jnp.bfloat16)
    boundary = jnp.stack([input_grad, output_again])
    weight_grads = jnp.stack([grad_up, grad_down])
    return boundary, weight_grads
```

```python
import jax
import jax.numpy as jnp
from jax import lax
from jax.sharding import Mesh
from jax.sharding import PartitionSpec as P

gelu_scale = 0.7978845608028654
cubic_coef = 0.044715
f32 = jnp.float32
bf16 = jnp.bfloat16


def gelu_value(preact):
    inner = gelu_scale * (preact + cubic_coef * preact * preact * preact)
    return 0.5 * preact * (1.0 + jnp.tanh(inner))


def gelu_slope(preact):
    inner = gelu_scale * (preact + cubic_coef * preact * preact * preact)
    tangent = jnp.tanh(inner)
    return 0.5 * (1.0 + tangent) + 0.5 * preact * (1.0 - tangent * tangent) * gelu_scale * (
        1.0 + 3.0 * cubic_coef * preact * preact
    )


def swap(block, axis):
    return lax.ppermute(block, axis, [(0, 1), (1, 0)])


def gather_by_exchange(block, axes):
    count = lax.axis_size(axes)
    copies = jnp.broadcast_to(block[None], (count, *block.shape))
    return lax.all_to_all(copies, axes, 0, 0).reshape(-1, block.shape[1])


def sum_by_exchange(parts, axes):
    count = lax.axis_size(axes)
    blocks = parts.reshape(count, -1, parts.shape[1])
    return lax.all_to_all(blocks, axes, 0, 0).astype(f32).sum(0)


def per_device(activations, weights):
    panel = activations[0]
    weight = weights[0]
    leading = lax.axis_index("section") == 0
    core = lax.axis_index("core")
    gathered = gather_by_exchange(panel, ("z", "x_hi"))
    half = gathered.shape[0] // 2
    own_rows = lax.dynamic_slice_in_dim(gathered, core * half, half, 0)
    other_rows = lax.dynamic_slice_in_dim(gathered, (1 - core) * half, half, 0)

    other_part = jnp.dot(other_rows, weight, preferred_element_type=f32).astype(bf16)
    arrived = swap(other_part, "core")
    own_part = jnp.dot(own_rows, weight, preferred_element_type=f32)
    chip_part = (own_part + arrived.astype(f32)).astype(bf16)
    shares = sum_by_exchange(chip_part, "y")

    sending = jnp.where(leading, gelu_value(shares), shares).astype(bf16)
    received = swap(sending, "section").astype(f32)
    own_side = jnp.where(leading, received * gelu_slope(shares), received).astype(bf16)

    own_hidden = lax.all_gather(own_side, "y", axis=0, tiled=True)
    other_hidden = swap(own_hidden, "core")

    def boundary_part(hidden):
        return lax.dot_general(hidden, weight, (((1,), (1,)), ((), ())), preferred_element_type=f32).astype(bf16)

    def grad_part(rows, hidden):
        return lax.dot_general(rows, hidden, (((0,), (0,)), ((), ())), preferred_element_type=f32)

    own_result = boundary_part(own_hidden)
    own_grad = grad_part(own_rows, own_hidden)
    other_result = boundary_part(other_hidden)
    first = core == 0
    partial = jnp.concatenate(
        [jnp.where(first, own_result, other_result), jnp.where(first, other_result, own_result)], axis=0
    )
    result = sum_by_exchange(partial, ("z", "x_hi")).astype(bf16)
    weight_grad = (own_grad + grad_part(other_rows, other_hidden)).astype(bf16)
    return (result[None], weight_grad[None])


def solution(mesh):
    sections, rows, cols = mesh.devices.shape
    fine = Mesh(
        mesh.devices.reshape(sections, rows // 2, 2, cols // 2, 2), ("section", "y", "core", "z", "x_hi")
    )
    by_token = P("section", ("z", "x_hi"), ("y", "core"))
    by_weight = P("section", ("y", "core"), ("z", "x_hi"))
    return jax.shard_map(
        per_device,
        mesh=fine,
        in_specs=(by_token, by_weight),
        out_specs=(by_token, by_weight),
        check_vma=False,
    )
```

```python
import jax
import jax.numpy as jnp
from jax import lax
from jax.sharding import Mesh
from jax.sharding import PartitionSpec as P

gelu_scale = 0.7978845608028654
cubic_coef = 0.044715
f32 = jnp.float32
bf16 = jnp.bfloat16


def gelu_value(preact):
    inner = gelu_scale * (preact + cubic_coef * preact * preact * preact)
    return 0.5 * preact * (1.0 + jnp.tanh(inner))


def gelu_slope(preact):
    inner = gelu_scale * (preact + cubic_coef * preact * preact * preact)
    tangent = jnp.tanh(inner)
    return 0.5 * (1.0 + tangent) + 0.5 * preact * (1.0 - tangent * tangent) * gelu_scale * (
        1.0 + 3.0 * cubic_coef * preact * preact
    )


def swap(block, axis):
    return lax.ppermute(block, axis, [(0, 1), (1, 0)])


def gather_by_exchange(block, axes):
    count = lax.axis_size(axes)
    copies = jnp.broadcast_to(block[None], (count, *block.shape))
    return lax.all_to_all(copies, axes, 0, 0).reshape(-1, block.shape[1])


def sum_by_exchange(parts, axes):
    count = lax.axis_size(axes)
    blocks = parts.reshape(count, -1, parts.shape[1])
    return lax.all_to_all(blocks, axes, 0, 0).astype(f32).sum(0)


def per_device(activations, weights):
    panel = activations[0]
    weight = weights[0]
    core = lax.axis_index("core")
    gathered = gather_by_exchange(panel, ("z", "x_hi"))
    half = gathered.shape[0] // 2
    own_rows = lax.dynamic_slice_in_dim(gathered, core * half, half, 0)
    other_rows = lax.dynamic_slice_in_dim(gathered, (1 - core) * half, half, 0)

    other_part = jnp.dot(other_rows, weight, preferred_element_type=f32).astype(bf16)
    arrived = swap(other_part, "core")
    own_part = jnp.dot(own_rows, weight, preferred_element_type=f32)
    chip_part = (own_part + arrived.astype(f32)).astype(bf16)
    pairs = lax.axis_size("y")
    blocks = lax.all_to_all(chip_part.reshape(2 * pairs, -1, chip_part.shape[1]), ("section", "y"), 0, 0)
    preact = blocks[:pairs].astype(f32).sum(0)
    dhidden = blocks[pairs:].astype(f32).sum(0).astype(bf16).astype(f32)
    hidden = gelu_value(preact).astype(bf16)
    dpre = (dhidden * gelu_slope(preact)).astype(bf16)
    sending = jnp.concatenate([jnp.broadcast_to(side[None], (pairs, *side.shape)) for side in (dpre, hidden)], axis=0)
    own_hidden = lax.all_to_all(sending, ("section", "y"), 0, 0).reshape(half, -1)
    other_hidden = swap(own_hidden, "core")

    def boundary_part(hidden):
        return lax.dot_general(hidden, weight, (((1,), (1,)), ((), ())), preferred_element_type=f32).astype(bf16)

    def grad_part(rows, hidden):
        return lax.dot_general(rows, hidden, (((0,), (0,)), ((), ())), preferred_element_type=f32)

    own_result = boundary_part(own_hidden)
    own_grad = grad_part(own_rows, own_hidden)
    other_result = boundary_part(other_hidden)
    first = core == 0
    partial = jnp.concatenate(
        [jnp.where(first, own_result, other_result), jnp.where(first, other_result, own_result)], axis=0
    )
    result = sum_by_exchange(partial, ("z", "x_hi")).astype(bf16)
    weight_grad = (own_grad + grad_part(other_rows, other_hidden)).astype(bf16)
    return (result[None], weight_grad[None])


def solution(mesh):
    sections, rows, cols = mesh.devices.shape
    fine = Mesh(
        mesh.devices.reshape(sections, rows // 2, 2, cols // 2, 2), ("section", "y", "core", "z", "x_hi")
    )
    by_token = P("section", ("z", "x_hi"), ("y", "core"))
    by_weight = P("section", ("y", "core"), ("z", "x_hi"))
    return jax.shard_map(
        per_device,
        mesh=fine,
        in_specs=(by_token, by_weight),
        out_specs=(by_token, by_weight),
        check_vma=False,
    )
```

```python
import jax
import jax.numpy as jnp
from jax import lax
from jax.sharding import Mesh
from jax.sharding import PartitionSpec as P

gelu_scale = 0.7978845608028654
cubic_coef = 0.044715
f32 = jnp.float32
bf16 = jnp.bfloat16
every_axis = ("section", "y", "core", "z", "x_hi")
chip_cols = ("core", "z", "x_hi")
lead = ("section", "y")


def gelu_value(preact):
    inner = gelu_scale * (preact + cubic_coef * preact * preact * preact)
    return 0.5 * preact * (1.0 + jnp.tanh(inner))


def gelu_slope(preact):
    inner = gelu_scale * (preact + cubic_coef * preact * preact * preact)
    tangent = jnp.tanh(inner)
    return 0.5 * (1.0 + tangent) + 0.5 * preact * (1.0 - tangent * tangent) * gelu_scale * (
        1.0 + 3.0 * cubic_coef * preact * preact
    )


def swap(block, axis):
    return lax.ppermute(block, axis, [(0, 1), (1, 0)])


def dot(left, right):
    return jnp.dot(left, right, preferred_element_type=f32)


def dot_t(left, right):
    return lax.dot_general(left, right, (((1,), (1,)), ((), ())), preferred_element_type=f32)


def grad_dot(rows, hidden):
    return lax.dot_general(rows, hidden, (((0,), (0,)), ((), ())), preferred_element_type=f32)


def per_device(activations, weights):
    panel = activations[0]
    weight = weights[0]
    core = lax.axis_index("core")
    cols = lax.axis_size("z") * lax.axis_size("x_hi")
    pairs = lax.axis_size("y")
    share = panel.shape[0] // 2
    width = panel.shape[1]

    out_panels = jnp.broadcast_to(panel.reshape(2, 1, share, width), (2, cols, share, width))
    gathered = lax.all_to_all(out_panels.reshape(2 * cols, share, width), chip_cols, 0, 0).reshape(2, cols * share, width)
    step = weight.shape[0] // 3
    both = jnp.concatenate([lax.all_gather(weight[at * step : (at + 1) * step], "core") for at in range(3)], axis=1)
    chip_part = (dot(gathered[0], both[0]) + dot(gathered[1], both[1])).astype(bf16)

    blocks = lax.all_to_all(chip_part.reshape(2 * pairs, -1, chip_part.shape[1]), lead, 0, 0)
    preact = blocks[:pairs].astype(f32).sum(0)
    dhidden = blocks[pairs:].astype(f32).sum(0).astype(bf16).astype(f32)
    hidden = gelu_value(preact).astype(bf16)
    dpre = (dhidden * gelu_slope(preact)).astype(bf16)
    sending = jnp.concatenate([jnp.broadcast_to(side[None], (pairs, *side.shape)) for side in (dpre, hidden)], axis=0)
    side = lax.all_to_all(sending, lead, 0, 0).reshape(cols * share, -1)

    partial = jnp.stack([dot_t(side, both[at]).astype(bf16) for at in range(2)])
    arrived = lax.all_to_all(partial.reshape(2 * cols, share, width), chip_cols, 0, 0)

    late_gathered, late_side = lax.optimization_barrier((gathered, side))
    late_own = lax.dynamic_index_in_dim(late_gathered, core, 0, False)
    late_other = swap(lax.dynamic_index_in_dim(late_gathered, 1 - core, 0, False), "core")
    rows = late_side.shape[0] // 2
    other_side = jnp.concatenate([swap(late_side[at * rows : (at + 1) * rows], "core") for at in range(2)], axis=0)
    weight_grad = (grad_dot(late_own, late_side) + grad_dot(late_other, other_side)).astype(bf16)
    arrived, weight_grad = lax.optimization_barrier((arrived, weight_grad))
    result = arrived.reshape(2, cols, share, width).astype(f32).sum(1).astype(bf16).reshape(2 * share, width)
    return (result[None], weight_grad[None])


def solution(mesh):
    sections, rows, cols = mesh.devices.shape
    fine = Mesh(mesh.devices.reshape(sections, rows // 2, 2, cols // 2, 2), every_axis)
    by_token = P("section", ("z", "x_hi"), ("y", "core"))
    by_weight = P("section", ("y", "core"), ("z", "x_hi"))
    return jax.shard_map(
        per_device,
        mesh=fine,
        in_specs=(by_token, by_weight),
        out_specs=(by_token, by_weight),
        check_vma=False,
    )
```

```python
import jax
import jax.numpy as jnp
from jax import lax
from jax.sharding import Mesh
from jax.sharding import PartitionSpec as P

gelu_scale = 0.7978845608028654
cubic_coef = 0.044715
f32 = jnp.float32
bf16 = jnp.bfloat16
every_axis = ("section", "y", "core", "z", "x_hi")
chip_cols = ("core", "z", "x_hi")
lead = ("section", "y")


def gelu_value(preact):
    inner = gelu_scale * (preact + cubic_coef * preact * preact * preact)
    return 0.5 * preact * (1.0 + jnp.tanh(inner))


def gelu_slope(preact):
    inner = gelu_scale * (preact + cubic_coef * preact * preact * preact)
    tangent = jnp.tanh(inner)
    return 0.5 * (1.0 + tangent) + 0.5 * preact * (1.0 - tangent * tangent) * gelu_scale * (
        1.0 + 3.0 * cubic_coef * preact * preact
    )


def swap(block, axis):
    return lax.ppermute(block, axis, [(0, 1), (1, 0)])


def dot(left, right):
    return jnp.dot(left, right, preferred_element_type=f32)


def dot_t(left, right):
    return lax.dot_general(left, right, (((1,), (1,)), ((), ())), preferred_element_type=f32)


def grad_dot(rows, hidden):
    return lax.dot_general(rows, hidden, (((0,), (0,)), ((), ())), preferred_element_type=f32)


def per_device(activations, weights):
    panel = activations[0]
    weight = weights[0]
    core = lax.axis_index("core").astype(jnp.uint32)
    cols = lax.axis_size("z") * lax.axis_size("x_hi")
    pairs = lax.axis_size("y")
    panel, core, other_core = lax.optimization_barrier((panel, core, 1 - core))
    share = panel.shape[0] // 2
    width = panel.shape[1]

    out_panels = jnp.broadcast_to(panel.reshape(2, 1, share, width), (2, cols, share, width))
    gathered = lax.all_to_all(out_panels.reshape(2 * cols, share, width), chip_cols, 0, 0).reshape(2, cols * share, width)
    step = weight.shape[0] // 3
    both = jnp.concatenate([lax.all_gather(weight[at * step : (at + 1) * step], "core") for at in range(3)], axis=1)
    chip_part = (dot(gathered[0], both[0]) + dot(gathered[1], both[1])).astype(bf16)

    blocks = lax.all_to_all(chip_part.reshape(2 * pairs, -1, chip_part.shape[1]), lead, 0, 0)
    preact = blocks[:pairs].astype(f32).sum(0)
    dhidden = blocks[pairs:].astype(f32).sum(0).astype(bf16).astype(f32)
    hidden = gelu_value(preact).astype(bf16)
    dpre = (dhidden * gelu_slope(preact)).astype(bf16)
    sending = jnp.concatenate([jnp.broadcast_to(side[None], (pairs, *side.shape)) for side in (dpre, hidden)], axis=0)
    side = lax.all_to_all(sending, lead, 0, 0).reshape(cols * share, -1)

    partial = lax.dot_general(both, side, (((2,), (1,)), ((), ())), preferred_element_type=f32).astype(bf16).transpose(0, 2, 1)
    arrived = lax.all_to_all(partial.reshape(2 * cols, share, width), chip_cols, 0, 0)

    late_gathered, late_side = lax.optimization_barrier((gathered, side))
    late_own = lax.dynamic_slice(late_gathered, (core, jnp.uint32(0), jnp.uint32(0)), (1, *late_gathered.shape[1:]))[0]
    late_other = lax.dynamic_slice(late_gathered, (other_core, jnp.uint32(0), jnp.uint32(0)), (1, *late_gathered.shape[1:]))[0]
    late_other = swap(late_other, "core")
    rows = late_side.shape[0] // 2
    other_side = jnp.concatenate([swap(late_side[at * rows : (at + 1) * rows], "core") for at in range(2)], axis=0)
    weight_grad = (grad_dot(late_own, late_side) + grad_dot(late_other, other_side)).astype(bf16)
    arrived, weight_grad = lax.optimization_barrier((arrived, weight_grad))
    result = arrived.reshape(2, cols, share, width).astype(f32).sum(1).astype(bf16).reshape(2 * share, width)
    return (result[None], weight_grad[None])


def solution(mesh):
    sections, rows, cols = mesh.devices.shape
    fine = Mesh(mesh.devices.reshape(sections, rows // 2, 2, cols // 2, 2), every_axis)
    by_token = P("section", ("z", "x_hi"), ("y", "core"))
    by_weight = P("section", ("y", "core"), ("z", "x_hi"))
    return jax.shard_map(
        per_device,
        mesh=fine,
        in_specs=(by_token, by_weight),
        out_specs=(by_token, by_weight),
        check_vma=False,
    )
```

```python
import jax
import jax.numpy as jnp
from jax import lax
from jax.sharding import Mesh
from jax.sharding import PartitionSpec as P

gelu_scale = 0.7978845608028654
cubic_coef = 0.044715
f32 = jnp.float32
bf16 = jnp.bfloat16
every_axis = ("section", "y", "core", "z", "x_hi")
chip_cols = ("core", "z", "x_hi")
lead = ("section", "y")


def gelu_value(preact):
    inner = gelu_scale * (preact + cubic_coef * preact * preact * preact)
    return 0.5 * preact * (1.0 + jnp.tanh(inner))


def gelu_slope(preact):
    inner = gelu_scale * (preact + cubic_coef * preact * preact * preact)
    tangent = jnp.tanh(inner)
    return 0.5 * (1.0 + tangent) + 0.5 * preact * (1.0 - tangent * tangent) * gelu_scale * (
        1.0 + 3.0 * cubic_coef * preact * preact
    )


def swap(block, axis):
    return lax.ppermute(block, axis, [(0, 1), (1, 0)])


def dot(left, right):
    return jnp.dot(left, right, preferred_element_type=f32)


def dot_t(left, right):
    return lax.dot_general(left, right, (((1,), (1,)), ((), ())), preferred_element_type=f32)


def grad_dot(rows, hidden):
    return lax.dot_general(rows, hidden, (((0,), (0,)), ((), ())), preferred_element_type=f32)


def per_device(activations, weights):
    panel = activations[0]
    weight = weights[0]
    core = lax.axis_index("core").astype(jnp.uint32)
    cols = lax.axis_size("z") * lax.axis_size("x_hi")
    pairs = lax.axis_size("y")
    panel, core, other_core = lax.optimization_barrier((panel, core, 1 - core))
    share = panel.shape[0] // 2
    width = panel.shape[1]

    out_panels = jnp.broadcast_to(panel.reshape(2, 1, share, width), (2, cols, share, width))
    gathered = lax.all_to_all(out_panels.reshape(2 * cols, share, width), chip_cols, 0, 0).reshape(2, cols * share, width)
    step = weight.shape[0] // 3
    both = jnp.concatenate([lax.all_gather(weight[at * step : (at + 1) * step], "core") for at in range(3)], axis=1)
    chip_part = lax.dot_general(gathered, both, (((0, 2), (0, 1)), ((), ())), preferred_element_type=f32).astype(bf16)

    blocks = lax.all_to_all(chip_part.reshape(2 * pairs, -1, chip_part.shape[1]), lead, 0, 0)
    preact = blocks[:pairs].astype(f32).sum(0)
    dhidden = blocks[pairs:].astype(f32).sum(0).astype(bf16).astype(f32)
    hidden = gelu_value(preact).astype(bf16)
    dpre = (dhidden * gelu_slope(preact)).astype(bf16)
    sending = jnp.concatenate([jnp.broadcast_to(side[None], (pairs, *side.shape)) for side in (dpre, hidden)], axis=0)
    side = lax.all_to_all(sending, lead, 0, 0).reshape(cols * share, -1)

    partial = lax.dot_general(both, side, (((2,), (1,)), ((), ())), preferred_element_type=f32).astype(bf16).transpose(0, 2, 1)
    arrived = lax.all_to_all(partial.reshape(2 * cols, share, width), chip_cols, 0, 0)

    late_gathered, late_side = lax.optimization_barrier((gathered, side))
    late_own = lax.dynamic_slice(late_gathered, (core, jnp.uint32(0), jnp.uint32(0)), (1, *late_gathered.shape[1:]))[0]
    late_other = lax.dynamic_slice(late_gathered, (other_core, jnp.uint32(0), jnp.uint32(0)), (1, *late_gathered.shape[1:]))[0]
    late_other = swap(late_other, "core")
    rows = late_side.shape[0] // 2
    other_side = jnp.concatenate([swap(late_side[at * rows : (at + 1) * rows], "core") for at in range(2)], axis=0)
    weight_grad = (grad_dot(late_own, late_side) + grad_dot(late_other, other_side)).astype(bf16)
    arrived, weight_grad = lax.optimization_barrier((arrived, weight_grad))
    result = arrived.reshape(2, cols, share, width).astype(f32).sum(1).astype(bf16).reshape(2 * share, width)
    return (result[None], weight_grad[None])


def solution(mesh):
    sections, rows, cols = mesh.devices.shape
    fine = Mesh(mesh.devices.reshape(sections, rows // 2, 2, cols // 2, 2), every_axis)
    by_token = P("section", ("z", "x_hi"), ("y", "core"))
    by_weight = P("section", ("y", "core"), ("z", "x_hi"))
    return jax.shard_map(
        per_device,
        mesh=fine,
        in_specs=(by_token, by_weight),
        out_specs=(by_token, by_weight),
        check_vma=False,
    )
```

```python
import jax
import jax.numpy as jnp
from jax import lax
from jax.sharding import Mesh
from jax.sharding import PartitionSpec as P

gelu_scale = 0.7978845608028654
cubic_coef = 0.044715
f32 = jnp.float32
bf16 = jnp.bfloat16
every_axis = ("section", "y", "core", "z", "x_hi")
chip_cols = ("core", "z", "x_hi")
lead = ("section", "y")


def gelu_value(preact):
    inner = gelu_scale * (preact + cubic_coef * preact * preact * preact)
    return 0.5 * preact * (1.0 + jnp.tanh(inner))


def gelu_slope(preact):
    inner = gelu_scale * (preact + cubic_coef * preact * preact * preact)
    tangent = jnp.tanh(inner)
    return 0.5 * (1.0 + tangent) + 0.5 * preact * (1.0 - tangent * tangent) * gelu_scale * (
        1.0 + 3.0 * cubic_coef * preact * preact
    )


def swap(block, axis):
    return lax.ppermute(block, axis, [(0, 1), (1, 0)])


def dot(left, right):
    return jnp.dot(left, right, preferred_element_type=f32)


def dot_t(left, right):
    return lax.dot_general(left, right, (((1,), (1,)), ((), ())), preferred_element_type=f32)


def grad_dot(rows, hidden):
    return lax.dot_general(rows, hidden, (((0,), (0,)), ((), ())), preferred_element_type=f32)


def over_rows(blocks):
    chips = lax.axis_size("y")
    others = 2 * lax.axis_size("z") * lax.axis_size("x_hi")
    order = [((section + 0) % 2, (at + 4) % chips) for section in range(2) for at in range(chips)]
    groups = [[(section * chips + chip) * others + at for section, chip in order] for at in range(others)]
    return lax.all_to_all(blocks, every_axis, 0, 0, axis_index_groups=groups)


def over_cols(blocks):
    deep = lax.axis_size("z")
    across = deep * 2
    order = [(core * deep + (at + 5) % deep) * 2 + (side + 1) % 2 for core in range(2) for at in range(deep) for side in range(2)]
    chips = lax.axis_size("section") * lax.axis_size("y")
    groups = [[chip * 2 * across + at for at in order] for chip in range(chips)]
    return lax.all_to_all(blocks, every_axis, 0, 0, axis_index_groups=groups)


def per_device(activations, weights):
    panel = activations[0]
    weight = weights[0]
    core = lax.axis_index("core").astype(jnp.uint32)
    cols = lax.axis_size("z") * lax.axis_size("x_hi")
    pairs = lax.axis_size("y")
    panel, core, other_core = lax.optimization_barrier((panel, core, 1 - core))
    share = panel.shape[0] // 2
    width = panel.shape[1]

    out_panels = jnp.broadcast_to(panel.reshape(2, 1, share, width), (2, cols, share, width))
    gathered = over_cols(out_panels.reshape(2 * cols, share, width)).reshape(2, cols * share, width)
    step = weight.shape[0] // 3
    both = jnp.concatenate([lax.all_gather(weight[at * step : (at + 1) * step], "core") for at in range(3)], axis=1)
    chip_part = lax.dot_general(gathered, both, (((0, 2), (0, 1)), ((), ())), preferred_element_type=f32).astype(bf16)

    blocks = over_rows(chip_part.reshape(2 * pairs, -1, chip_part.shape[1]))
    preact = blocks[:pairs].astype(f32).sum(0)
    dhidden = blocks[pairs:].astype(f32).sum(0).astype(bf16).astype(f32)
    hidden = gelu_value(preact).astype(bf16)
    dpre = (dhidden * gelu_slope(preact)).astype(bf16)
    sending = jnp.concatenate([jnp.broadcast_to(side[None], (pairs, *side.shape)) for side in (dpre, hidden)], axis=0)
    side = over_rows(sending).reshape(cols * share, -1)

    partial = lax.dot_general(both, side, (((2,), (1,)), ((), ())), preferred_element_type=f32).astype(bf16).transpose(0, 2, 1)
    arrived = over_cols(partial.reshape(2 * cols, share, width))

    late_gathered, late_side = lax.optimization_barrier((gathered, side))
    late_own = lax.dynamic_slice(late_gathered, (core, jnp.uint32(0), jnp.uint32(0)), (1, *late_gathered.shape[1:]))[0]
    late_other = lax.dynamic_slice(late_gathered, (other_core, jnp.uint32(0), jnp.uint32(0)), (1, *late_gathered.shape[1:]))[0]
    late_other = swap(late_other, "core")
    rows = late_side.shape[0] // 2
    other_side = jnp.concatenate([swap(late_side[at * rows : (at + 1) * rows], "core") for at in range(2)], axis=0)
    weight_grad = (grad_dot(late_own, late_side) + grad_dot(late_other, other_side)).astype(bf16)
    arrived, weight_grad = lax.optimization_barrier((arrived, weight_grad))
    result = arrived.reshape(2, cols, share, width).astype(f32).sum(1).astype(bf16).reshape(2 * share, width)
    return (result[None], weight_grad[None])


def solution(mesh):
    sections, rows, cols = mesh.devices.shape
    fine = Mesh(mesh.devices.reshape(sections, rows // 2, 2, cols // 2, 2), every_axis)
    by_token = P("section", ("z", "x_hi"), ("y", "core"))
    by_weight = P("section", ("y", "core"), ("z", "x_hi"))
    return jax.shard_map(
        per_device,
        mesh=fine,
        in_specs=(by_token, by_weight),
        out_specs=(by_token, by_weight),
        check_vma=False,
    )
```

```python
import jax
import jax.numpy as jnp
from jax import lax
from jax.sharding import Mesh
from jax.sharding import PartitionSpec as P

gelu_scale = 0.7978845608028654
cubic_coef = 0.044715
f32 = jnp.float32
bf16 = jnp.bfloat16
every_axis = ("section", "y", "core", "z", "x_hi")
chip_cols = ("core", "z", "x_hi")
lead = ("section", "y")


def gelu_value(preact):
    inner = gelu_scale * (preact + cubic_coef * preact * preact * preact)
    return 0.5 * preact * (1.0 + jnp.tanh(inner))


def gelu_slope(preact):
    inner = gelu_scale * (preact + cubic_coef * preact * preact * preact)
    tangent = jnp.tanh(inner)
    return 0.5 * (1.0 + tangent) + 0.5 * preact * (1.0 - tangent * tangent) * gelu_scale * (
        1.0 + 3.0 * cubic_coef * preact * preact
    )


def swap(block, axis):
    return lax.ppermute(block, axis, [(0, 1), (1, 0)])


def dot(left, right):
    return jnp.dot(left, right, preferred_element_type=f32)


def dot_t(left, right):
    return lax.dot_general(left, right, (((1,), (1,)), ((), ())), preferred_element_type=f32)


def grad_dot(rows, hidden):
    return lax.dot_general(rows, hidden, (((0,), (0,)), ((), ())), preferred_element_type=f32)


def over_rows(blocks):
    chips = lax.axis_size("y")
    others = 2 * lax.axis_size("z") * lax.axis_size("x_hi")
    order = [(section, (4 + (at // 2 if at % 2 == 0 else -(at + 1) // 2)) % chips) for section in range(2) for at in range(chips)]
    groups = [[(section * chips + chip) * others + at for section, chip in order] for at in range(others)]
    return lax.all_to_all(blocks, every_axis, 0, 0, axis_index_groups=groups)


def over_cols(blocks):
    deep = lax.axis_size("z")
    across = deep * 2
    order = [(core * deep + (at + 5) % deep) * 2 + (side + 1) % 2 for core in range(2) for at in range(deep) for side in range(2)]
    chips = lax.axis_size("section") * lax.axis_size("y")
    groups = [[chip * 2 * across + at for at in order] for chip in range(chips)]
    return lax.all_to_all(blocks, every_axis, 0, 0, axis_index_groups=groups)


def per_device(activations, weights):
    panel = activations[0]
    weight = weights[0]
    core = lax.axis_index("core").astype(jnp.uint32)
    cols = lax.axis_size("z") * lax.axis_size("x_hi")
    pairs = lax.axis_size("y")
    panel, core, other_core = lax.optimization_barrier((panel, core, 1 - core))
    share = panel.shape[0] // 2
    width = panel.shape[1]

    out_panels = jnp.broadcast_to(panel.reshape(2, 1, share, width), (2, cols, share, width))
    gathered = over_cols(out_panels.reshape(2 * cols, share, width)).reshape(2, cols * share, width)
    step = weight.shape[0] // 3
    both = jnp.concatenate([lax.all_gather(weight[at * step : (at + 1) * step], "core") for at in range(3)], axis=1)
    chip_part = lax.dot_general(gathered, both, (((0, 2), (0, 1)), ((), ())), preferred_element_type=f32).astype(bf16)

    blocks = over_rows(chip_part.reshape(2 * pairs, -1, chip_part.shape[1]))
    preact = blocks[:pairs].astype(f32).sum(0)
    dhidden = blocks[pairs:].astype(f32).sum(0).astype(bf16).astype(f32)
    hidden = gelu_value(preact).astype(bf16)
    dpre = (dhidden * gelu_slope(preact)).astype(bf16)
    sending = jnp.concatenate([jnp.broadcast_to(side[None], (pairs, *side.shape)) for side in (dpre, hidden)], axis=0)
    side = over_rows(sending).reshape(cols * share, -1)

    partial = lax.dot_general(both, side, (((2,), (1,)), ((), ())), preferred_element_type=f32).astype(bf16).transpose(0, 2, 1)
    arrived = over_cols(partial.reshape(2 * cols, share, width))

    late_gathered, late_side = lax.optimization_barrier((gathered, side))
    late_own = lax.dynamic_slice(late_gathered, (core, jnp.uint32(0), jnp.uint32(0)), (1, *late_gathered.shape[1:]))[0]
    late_other = lax.dynamic_slice(late_gathered, (other_core, jnp.uint32(0), jnp.uint32(0)), (1, *late_gathered.shape[1:]))[0]
    late_other = swap(late_other, "core")
    rows = late_side.shape[0] // 2
    other_side = jnp.concatenate([swap(late_side[at * rows : (at + 1) * rows], "core") for at in range(2)], axis=0)
    weight_grad = (grad_dot(late_own, late_side) + grad_dot(late_other, other_side)).astype(bf16)
    arrived, weight_grad = lax.optimization_barrier((arrived, weight_grad))
    result = arrived.reshape(2, cols, share, width).astype(f32).sum(1).astype(bf16).reshape(2 * share, width)
    return (result[None], weight_grad[None])


def solution(mesh):
    sections, rows, cols = mesh.devices.shape
    fine = Mesh(mesh.devices.reshape(sections, rows // 2, 2, cols // 2, 2), every_axis)
    by_token = P("section", ("z", "x_hi"), ("y", "core"))
    by_weight = P("section", ("y", "core"), ("z", "x_hi"))
    return jax.shard_map(
        per_device,
        mesh=fine,
        in_specs=(by_token, by_weight),
        out_specs=(by_token, by_weight),
        check_vma=False,
    )
```

```python
import jax
import jax.numpy as jnp
from jax import lax
from jax.sharding import Mesh
from jax.sharding import PartitionSpec as P

gelu_scale = 0.7978845608028654
cubic_coef = 0.044715
f32 = jnp.float32
bf16 = jnp.bfloat16
every_axis = ("section", "y", "core", "z", "x_hi")
chip_cols = ("core", "z", "x_hi")
lead = ("section", "y")


def gelu_value(preact):
    inner = gelu_scale * (preact + cubic_coef * preact * preact * preact)
    return 0.5 * preact * (1.0 + jnp.tanh(inner))


def gelu_slope(preact):
    inner = gelu_scale * (preact + cubic_coef * preact * preact * preact)
    tangent = jnp.tanh(inner)
    return 0.5 * (1.0 + tangent) + 0.5 * preact * (1.0 - tangent * tangent) * gelu_scale * (
        1.0 + 3.0 * cubic_coef * preact * preact
    )


def swap(block, axis):
    return lax.ppermute(block, axis, [(0, 1), (1, 0)])


def dot(left, right):
    return jnp.dot(left, right, preferred_element_type=f32)


def dot_t(left, right):
    return lax.dot_general(left, right, (((1,), (1,)), ((), ())), preferred_element_type=f32)


def grad_dot(rows, hidden):
    return lax.dot_general(rows, hidden, (((0,), (0,)), ((), ())), preferred_element_type=f32)


def over_rows(blocks):
    chips = lax.axis_size("y")
    others = 2 * lax.axis_size("z") * lax.axis_size("x_hi")
    groups = []
    for at in range(others):
        first = (6, 4)[at // (others // 2)]
        groups.append(
            [(section * chips + (turn + first) % chips) * others + at for section in range(2) for turn in range(chips)]
        )
    return lax.all_to_all(blocks, every_axis, 0, 0, axis_index_groups=groups)


def over_cols(blocks):
    deep = lax.axis_size("z")
    across = deep * 2
    order = [(core * deep + (at + 5) % deep) * 2 + (side + 1) % 2 for core in range(2) for at in range(deep) for side in range(2)]
    chips = lax.axis_size("section") * lax.axis_size("y")
    groups = [[chip * 2 * across + at for at in order] for chip in range(chips)]
    return lax.all_to_all(blocks, every_axis, 0, 0, axis_index_groups=groups)


def per_device(activations, weights):
    panel = activations[0]
    weight = weights[0]
    core = lax.axis_index("core").astype(jnp.uint32)
    cols = lax.axis_size("z") * lax.axis_size("x_hi")
    pairs = lax.axis_size("y")
    panel, core, other_core = lax.optimization_barrier((panel, core, 1 - core))
    share = panel.shape[0] // 2
    width = panel.shape[1]

    out_panels = jnp.broadcast_to(panel.reshape(2, 1, share, width), (2, cols, share, width))
    gathered = over_cols(out_panels.reshape(2 * cols, share, width)).reshape(2, cols * share, width)
    step = weight.shape[0] // 3
    both = jnp.concatenate([lax.all_gather(weight[at * step : (at + 1) * step], "core") for at in range(3)], axis=1)
    chip_part = lax.dot_general(gathered, both, (((0, 2), (0, 1)), ((), ())), preferred_element_type=f32).astype(bf16)

    blocks = over_rows(chip_part.reshape(2 * pairs, -1, chip_part.shape[1]))
    preact = blocks[:pairs].astype(f32).sum(0)
    dhidden = blocks[pairs:].astype(f32).sum(0).astype(bf16).astype(f32)
    hidden = gelu_value(preact).astype(bf16)
    dpre = (dhidden * gelu_slope(preact)).astype(bf16)
    sending = jnp.concatenate([jnp.broadcast_to(side[None], (pairs, *side.shape)) for side in (dpre, hidden)], axis=0)
    side = over_rows(sending).reshape(cols * share, -1)

    partial = lax.dot_general(both, side, (((2,), (1,)), ((), ())), preferred_element_type=f32).astype(bf16).transpose(0, 2, 1)
    arrived = over_cols(partial.reshape(2 * cols, share, width))

    late_gathered, late_side = lax.optimization_barrier((gathered, side))
    late_own = lax.dynamic_slice(late_gathered, (core, jnp.uint32(0), jnp.uint32(0)), (1, *late_gathered.shape[1:]))[0]
    late_other = lax.dynamic_slice(late_gathered, (other_core, jnp.uint32(0), jnp.uint32(0)), (1, *late_gathered.shape[1:]))[0]
    late_other = swap(late_other, "core")
    rows = late_side.shape[0] // 2
    other_side = jnp.concatenate([swap(late_side[at * rows : (at + 1) * rows], "core") for at in range(2)], axis=0)
    weight_grad = (grad_dot(late_own, late_side) + grad_dot(late_other, other_side)).astype(bf16)
    arrived, weight_grad = lax.optimization_barrier((arrived, weight_grad))
    result = arrived.reshape(2, cols, share, width).astype(f32).sum(1).astype(bf16).reshape(2 * share, width)
    return (result[None], weight_grad[None])


def solution(mesh):
    sections, rows, cols = mesh.devices.shape
    fine = Mesh(mesh.devices.reshape(sections, rows // 2, 2, cols // 2, 2), every_axis)
    by_token = P("section", ("z", "x_hi"), ("y", "core"))
    by_weight = P("section", ("y", "core"), ("z", "x_hi"))
    return jax.shard_map(
        per_device,
        mesh=fine,
        in_specs=(by_token, by_weight),
        out_specs=(by_token, by_weight),
        check_vma=False,
    )
```

```python
import jax
import jax.numpy as jnp
from jax import lax
from jax.sharding import Mesh
from jax.sharding import PartitionSpec as P

gelu_scale = 0.7978845608028654
cubic_coef = 0.044715
f32 = jnp.float32
bf16 = jnp.bfloat16
every_axis = ("section", "y", "core", "z", "x_hi")
chip_cols = ("core", "z", "x_hi")
lead = ("section", "y")


def gelu_value(preact):
    inner = gelu_scale * (preact + cubic_coef * preact * preact * preact)
    return 0.5 * preact * (1.0 + jnp.tanh(inner))


def gelu_slope(preact):
    inner = gelu_scale * (preact + cubic_coef * preact * preact * preact)
    tangent = jnp.tanh(inner)
    return 0.5 * (1.0 + tangent) + 0.5 * preact * (1.0 - tangent * tangent) * gelu_scale * (
        1.0 + 3.0 * cubic_coef * preact * preact
    )


def swap(block, axis):
    return lax.ppermute(block, axis, [(0, 1), (1, 0)])


def dot(left, right):
    return jnp.dot(left, right, preferred_element_type=f32)


def dot_t(left, right):
    return lax.dot_general(left, right, (((1,), (1,)), ((), ())), preferred_element_type=f32)


def grad_dot(rows, hidden):
    return lax.dot_general(rows, hidden, (((0,), (0,)), ((), ())), preferred_element_type=f32)


def over_rows(blocks):
    chips = lax.axis_size("y")
    others = 2 * lax.axis_size("z") * lax.axis_size("x_hi")
    groups = []
    for at in range(others):
        first = (6, 4)[at // (others // 2)]
        groups.append(
            [
                (section * chips + (first + (turn // 2 if turn % 2 == 0 else -(turn + 1) // 2)) % chips) * others + at
                for section in range(2)
                for turn in range(chips)
            ]
        )
    return lax.all_to_all(blocks, every_axis, 0, 0, axis_index_groups=groups)


def over_cols(blocks):
    deep = lax.axis_size("z")
    across = deep * 2
    order = [(core * deep + (at + 5) % deep) * 2 + (side + 1) % 2 for core in range(2) for at in range(deep) for side in range(2)]
    chips = lax.axis_size("section") * lax.axis_size("y")
    groups = [[chip * 2 * across + at for at in order] for chip in range(chips)]
    return lax.all_to_all(blocks, every_axis, 0, 0, axis_index_groups=groups)


def per_device(activations, weights):
    panel = activations[0]
    weight = weights[0]
    core = lax.axis_index("core").astype(jnp.uint32)
    cols = lax.axis_size("z") * lax.axis_size("x_hi")
    pairs = lax.axis_size("y")
    panel, core, other_core = lax.optimization_barrier((panel, core, 1 - core))
    share = panel.shape[0] // 2
    width = panel.shape[1]

    out_panels = jnp.broadcast_to(panel.reshape(2, 1, share, width), (2, cols, share, width))
    gathered = over_cols(out_panels.reshape(2 * cols, share, width)).reshape(2, cols * share, width)
    step = weight.shape[0] // 3
    both = jnp.concatenate([lax.all_gather(weight[at * step : (at + 1) * step], "core") for at in range(3)], axis=1)
    chip_part = lax.dot_general(gathered, both, (((0, 2), (0, 1)), ((), ())), preferred_element_type=f32).astype(bf16)

    blocks = over_rows(chip_part.reshape(2 * pairs, -1, chip_part.shape[1]))
    preact = blocks[:pairs].astype(f32).sum(0)
    dhidden = blocks[pairs:].astype(f32).sum(0).astype(bf16).astype(f32)
    hidden = gelu_value(preact).astype(bf16)
    dpre = (dhidden * gelu_slope(preact)).astype(bf16)
    sending = jnp.concatenate([jnp.broadcast_to(side[None], (pairs, *side.shape)) for side in (dpre, hidden)], axis=0)
    side = over_rows(sending).reshape(cols * share, -1)

    partial = lax.dot_general(both, side, (((2,), (1,)), ((), ())), preferred_element_type=f32).astype(bf16).transpose(0, 2, 1)
    arrived = over_cols(partial.reshape(2 * cols, share, width))

    late_gathered, late_side = lax.optimization_barrier((gathered, side))
    late_own = lax.dynamic_slice(late_gathered, (core, jnp.uint32(0), jnp.uint32(0)), (1, *late_gathered.shape[1:]))[0]
    late_other = lax.dynamic_slice(late_gathered, (other_core, jnp.uint32(0), jnp.uint32(0)), (1, *late_gathered.shape[1:]))[0]
    late_other = swap(late_other, "core")
    rows = late_side.shape[0] // 2
    other_side = jnp.concatenate([swap(late_side[at * rows : (at + 1) * rows], "core") for at in range(2)], axis=0)
    weight_grad = (grad_dot(late_own, late_side) + grad_dot(late_other, other_side)).astype(bf16)
    arrived, weight_grad = lax.optimization_barrier((arrived, weight_grad))
    result = arrived.reshape(2, cols, share, width).astype(f32).sum(1).astype(bf16).reshape(2 * share, width)
    return (result[None], weight_grad[None])


def solution(mesh):
    sections, rows, cols = mesh.devices.shape
    fine = Mesh(mesh.devices.reshape(sections, rows // 2, 2, cols // 2, 2), every_axis)
    by_token = P("section", ("z", "x_hi"), ("y", "core"))
    by_weight = P("section", ("y", "core"), ("z", "x_hi"))
    return jax.shard_map(
        per_device,
        mesh=fine,
        in_specs=(by_token, by_weight),
        out_specs=(by_token, by_weight),
        check_vma=False,
    )
```

```python
import jax
import jax.numpy as jnp
from jax import lax
from jax.sharding import Mesh
from jax.sharding import PartitionSpec as P

gelu_scale = 0.7978845608028654
cubic_coef = 0.044715
f32 = jnp.float32
bf16 = jnp.bfloat16
every_axis = ("section", "y", "core", "z", "x_hi")
chip_cols = ("core", "z", "x_hi")
lead = ("section", "y")


def gelu_value(preact):
    inner = gelu_scale * (preact + cubic_coef * preact * preact * preact)
    return 0.5 * preact * (1.0 + jnp.tanh(inner))


def gelu_slope(preact):
    inner = gelu_scale * (preact + cubic_coef * preact * preact * preact)
    tangent = jnp.tanh(inner)
    return 0.5 * (1.0 + tangent) + 0.5 * preact * (1.0 - tangent * tangent) * gelu_scale * (
        1.0 + 3.0 * cubic_coef * preact * preact
    )


def swap(block, axis):
    return lax.ppermute(block, axis, [(0, 1), (1, 0)])


def dot(left, right):
    return jnp.dot(left, right, preferred_element_type=f32)


def dot_t(left, right):
    return lax.dot_general(left, right, (((1,), (1,)), ((), ())), preferred_element_type=f32)


def grad_dot(rows, hidden):
    return lax.dot_general(rows, hidden, (((0,), (0,)), ((), ())), preferred_element_type=f32)


def over_rows(blocks):
    chips = lax.axis_size("y")
    others = 2 * lax.axis_size("z") * lax.axis_size("x_hi")
    groups = []
    for at in range(others):
        first = (6, 4)[at // (others // 2)]
        groups.append(
            [(section * chips + (turn + first) % chips) * others + at for section in range(2) for turn in range(chips)]
        )
    return lax.all_to_all(blocks, every_axis, 0, 0, axis_index_groups=groups)


def over_cols(blocks):
    deep = lax.axis_size("z")
    across = deep * 2
    order = [core * across + (at + 11) % across for core in range(2) for at in range(across)]
    chips = lax.axis_size("section") * lax.axis_size("y")
    groups = [[chip * 2 * across + at for at in order] for chip in range(chips)]
    return lax.all_to_all(blocks, every_axis, 0, 0, axis_index_groups=groups)


def per_device(activations, weights):
    panel = activations[0]
    weight = weights[0]
    core = lax.axis_index("core").astype(jnp.uint32)
    cols = lax.axis_size("z") * lax.axis_size("x_hi")
    pairs = lax.axis_size("y")
    panel, core, other_core = lax.optimization_barrier((panel, core, 1 - core))
    share = panel.shape[0] // 2
    width = panel.shape[1]

    out_panels = jnp.broadcast_to(panel.reshape(2, 1, share, width), (2, cols, share, width))
    gathered = over_cols(out_panels.reshape(2 * cols, share, width)).reshape(2, cols * share, width)
    step = weight.shape[0] // 3
    both = jnp.concatenate([lax.all_gather(weight[at * step : (at + 1) * step], "core") for at in range(3)], axis=1)
    chip_part = lax.dot_general(gathered, both, (((0, 2), (0, 1)), ((), ())), preferred_element_type=f32).astype(bf16)

    blocks = over_rows(chip_part.reshape(2 * pairs, -1, chip_part.shape[1]))
    preact = blocks[:pairs].astype(f32).sum(0)
    dhidden = blocks[pairs:].astype(f32).sum(0).astype(bf16).astype(f32)
    hidden = gelu_value(preact).astype(bf16)
    dpre = (dhidden * gelu_slope(preact)).astype(bf16)
    sending = jnp.concatenate([jnp.broadcast_to(side[None], (pairs, *side.shape)) for side in (dpre, hidden)], axis=0)
    side = over_rows(sending).reshape(cols * share, -1)

    partial = lax.dot_general(both, side, (((2,), (1,)), ((), ())), preferred_element_type=f32).astype(bf16).transpose(0, 2, 1)
    arrived = over_cols(partial.reshape(2 * cols, share, width))

    late_gathered, late_side = lax.optimization_barrier((gathered, side))
    late_own = lax.dynamic_slice(late_gathered, (core, jnp.uint32(0), jnp.uint32(0)), (1, *late_gathered.shape[1:]))[0]
    late_other = lax.dynamic_slice(late_gathered, (other_core, jnp.uint32(0), jnp.uint32(0)), (1, *late_gathered.shape[1:]))[0]
    late_other = swap(late_other, "core")
    rows = late_side.shape[0] // 2
    other_side = jnp.concatenate([swap(late_side[at * rows : (at + 1) * rows], "core") for at in range(2)], axis=0)
    weight_grad = (grad_dot(late_own, late_side) + grad_dot(late_other, other_side)).astype(bf16)
    arrived, weight_grad = lax.optimization_barrier((arrived, weight_grad))
    result = arrived.reshape(2, cols, share, width).astype(f32).sum(1).astype(bf16).reshape(2 * share, width)
    return (result[None], weight_grad[None])


def solution(mesh):
    sections, rows, cols = mesh.devices.shape
    fine = Mesh(mesh.devices.reshape(sections, rows // 2, 2, cols // 2, 2), every_axis)
    by_token = P("section", ("z", "x_hi"), ("y", "core"))
    by_weight = P("section", ("y", "core"), ("z", "x_hi"))
    return jax.shard_map(
        per_device,
        mesh=fine,
        in_specs=(by_token, by_weight),
        out_specs=(by_token, by_weight),
        check_vma=False,
    )
```
